256 devices in a mesh: tok: 32 (over z, x), col: 8 (over y, core).
Axes of the slice: x: 4, y: 4, z: 8, core: 2. Of those that a mesh axis runs over, the one named last changes fastest.
Arguments:
- inputs: bfloat16 [16384, 8192], P('tok'), may hold values from -6 to 6
- out_grads: bfloat16 [16384, 10240], P('tok', 'col'), may hold values from -0.046875 to 0.046875
- basis: bfloat16 [8192, 1024], P('tok'), may hold values from -0.0625 to 0.0625
- residual: bfloat16 [16384, 8192], P('tok', 'col')
- test_matrix: bfloat16 [8192, 256], P('col'), may hold values from -0.0625 to 0.0625
Outputs:
- weight_grad: bfloat16 [8192, 10240], P('tok', 'col')
- sketch_basis: float32 [8192, 256], P(('col', 'tok'))
The draws below stay inside these ranges and needn't reach their ends.
All inputs are finite; a program needn't handle non-finite values.
Results may differ from the reference program's by a relative error of at most 0.025.
Values may be sent and summed in bfloat16 or wider, within the bound.
No kernel may reach another device: no remote copies, remote signals or barrier semaphores. Data moves between devices by JAX's collectives and lax.ppermute only.
A program may use at most 128 MiB of HBM per device.

```python
import jax
import jax.numpy as jnp
from jax import lax

D = 8192
QKV = 10240
BASIS = 1024
SKETCH = 256
TOKENS = 16384
N_TOK = 32
N_COL = 8


def draw_residual(key, part):
    key = jax.random.fold_in(key, 7)
    key_values, key_cols = jax.random.split(key)
    ramp = jnp.exp(jnp.log(3.0) * jnp.arange(D, dtype=jnp.float32) / D)
    values = jax.random.normal(key_values, (TOKENS, D), jnp.float32)
    rough = jax.random.uniform(key_cols, (D,), jnp.float32, 0.6, 1.4)
    return (values * (ramp * rough)[None, :]).astype(jnp.bfloat16)


def strengthened(entries, stream_key, source, target, blocks, factor):
    owner, partner = [(jnp.arange(entries.shape[position]) // (entries.shape[position] // blocks)).reshape([-1 if axis == position else 1 for axis in range(entries.ndim)]) for position in (source, target)]
    chosen = jax.random.permutation(stream_key, blocks)[partner]
    strong = (owner == chosen) | (owner == (partner + blocks // 2) % blocks)
    return jnp.where(strong, factor * entries, entries)


def block_levels(own_key, extent, cuts, low, high):
    level, own = 1.0, jax.random.fold_in(own_key, 6)
    for dim, shards_of in cuts:
        steps = jnp.exp(jax.random.uniform(jax.random.fold_in(own, dim), (shards_of,), jnp.float32, low / len(cuts), high / len(cuts)))
        level = level * jnp.repeat(steps, extent[dim] // shards_of).reshape([-1 if axis == dim else 1 for axis in range(len(extent))])
    return level


def noise(key, dims, scale, bound, cuts=(), kind=jnp.bfloat16):
    entries = jax.random.normal(key, dims, jnp.float32) * scale
    if len(cuts) > 0:
        entries = block_levels(key, dims, cuts, -0.22, 0.18) * entries
    return jnp.clip(entries, min=-bound, max=bound).astype(kind)


def heavy_noise(rng, shape, scale, reach, pieces, heavy, held_as=jnp.bfloat16):
    entries = scale * jax.random.normal(rng, shape, jnp.float32)
    if pieces:
        entries = entries * block_levels(rng, shape, pieces, -0.22, 0.18)
    return jnp.clip(strengthened(entries, jax.random.fold_in(rng, 3), *heavy), -reach, reach).astype(held_as)


def setup_inputs(seed: int = 0) -> dict:
    streams_of = jax.random.split(jax.random.key(seed), 6)
    inputs = heavy_noise(streams_of[0], (TOKENS, D), 1.0, 6.0, ((0, 32),), (0, 1, 32, 2.75))
    out_grads = noise(streams_of[1], (TOKENS, QKV), TOKENS ** -0.5, 0.046875, ((0, 32), (1, 8)))
    basis = noise(streams_of[2], (D, BASIS), D ** -0.5, 0.0625, ((0, 32),))
    residual = draw_residual(jax.random.fold_in(streams_of[5], 71), 0)
    test_matrix = noise(streams_of[4], (D, SKETCH), D ** -0.5, 0.0625, ((0, 8),))
    return dict(inputs=inputs, out_grads=out_grads, basis=basis, residual=residual, test_matrix=test_matrix)


def reference(inputs, out_grads, basis, residual, test_matrix):
    shard = inputs.shape[0] // N_TOK
    panel = QKV // N_COL
    input_groups = inputs.reshape(N_TOK, shard, D)
    grad_groups = out_grads.reshape(N_TOK, shard, QKV)

    def column_block(offset):
        block = lax.dynamic_slice_in_dim(grad_groups, offset, panel, 2)

        def add_group(total, pair):
            left, right = pair
            part = lax.dot_general(left.astype(jnp.float32), right.astype(jnp.float32), (((0,), (0,)), ((), ())), preferred_element_type=jnp.float32)
            part = lax.optimization_barrier(part.astype(jnp.bfloat16)).astype(jnp.float32)
            return (total + part, None)
        total, unused = lax.scan(add_group, jnp.zeros((D, panel), jnp.float32), (input_groups, block))
        return total
    offsets = jnp.arange(N_COL, dtype=jnp.int32) * panel
    blocks = lax.map(column_block, offsets)
    grad = jnp.transpose(blocks, (1, 0, 2)).reshape(D, QKV)
    grad_low = grad.astype(jnp.bfloat16)
    coords = lax.dot_general(basis.astype(jnp.float32), grad_low.astype(jnp.float32), (((0,), (0,)), ((), ())), preferred_element_type=jnp.float32).astype(jnp.bfloat16)
    correction = jnp.dot(basis.astype(jnp.float32), coords.astype(jnp.float32), preferred_element_type=jnp.float32)
    weight_grad = (grad - correction).astype(jnp.bfloat16)
    probe = jnp.dot(residual.astype(jnp.float32), test_matrix.astype(jnp.float32), preferred_element_type=jnp.float32).astype(jnp.bfloat16)
    sketch = lax.dot_general(residual.astype(jnp.float32), probe.astype(jnp.float32), (((0,), (0,)), ((), ())), preferred_element_type=jnp.float32)
    gram = jnp.dot(sketch.T, sketch, precision=lax.Precision.HIGHEST) / D
    lower = jnp.linalg.cholesky(gram)
    sketch_basis = jax.scipy.linalg.solve_triangular(lower, sketch.T, lower=True).T
    return (weight_grad, sketch_basis)
```

```python
import jax
import jax.numpy as jnp
from jax import lax
from jax.sharding import Mesh, PartitionSpec as P

D = 8192
BF = jnp.bfloat16
F32 = jnp.float32
TOK = ("z", "x")
COL = ("y", "core")


def shift(a, axis, n, d):
    return lax.ppermute(a, axis, [(i, (i + d) % n) for i in range(n)])


def dot(a, b, ca, cb, **kw):
    return lax.dot_general(a, b, (((ca,), (cb,)), ((), ())), preferred_element_type=F32, **kw)


def exchange(a, axes):
    return lax.all_to_all(a, axes, split_axis=0, concat_axis=0, tiled=False)


def gather_small(a, axes, n):
    parts = exchange(jnp.broadcast_to(a[None], (n,) + a.shape), axes)
    return parts.reshape((n * a.shape[0],) + a.shape[1:])


def sum_small(a, axes, n):
    parts = exchange(a.reshape((n, a.shape[0] // n) + a.shape[1:]), axes)
    return jnp.sum(parts.astype(F32), axis=0)


def gather_ring4(a, axis):
    half = a.shape[0] // 2
    one = shift(a, axis, 4, 1)
    three = shift(a, axis, 4, -1)
    top = shift(one[:half], axis, 4, 1)
    bottom = shift(three[half:], axis, 4, -1)
    return [a, one, jnp.concatenate([top, bottom], axis=0), three]


def per_device(inputs, out_grads, basis, residual, test_matrix):
    z, x, y, core = (lax.axis_index(name) for name in ("z", "x", "y", "core"))
    col = 2 * y + core

    def block(d):
        return lax.dynamic_slice(inputs, (0, 1024 * col + 256 * ((x + d) % 4)), (512, 256))

    mine = jnp.concatenate([block(0)] + [shift(block(d), "x", 4, d) for d in (1, 2, 3)], axis=0)
    along_y = gather_ring4(mine, "y")
    pieces = []
    for piece in along_y:
        pieces += [piece, shift(piece, "core", 2, 1)]
    rows_of = jnp.concatenate(pieces, axis=1)
    grads = jnp.concatenate(gather_ring4(out_grads, "x"), axis=0)

    basis_rows = lax.all_gather(basis, "z", axis=0, tiled=True)
    basis_rows = jnp.concatenate(
        [
            lax.dynamic_slice(basis_rows, (256 * (2 * ((y - p // 2) % 4) + (core ^ (p % 2))), 0), (256, 1024))
            for p in range(8)
        ],
        axis=0,
    )

    grad_t = lax.psum_scatter(dot(grads, rows_of, 0, 0).astype(BF), "z", scatter_dimension=0, tiled=True)
    part = dot(grad_t, basis_rows, 1, 0).astype(BF)
    coords = part.astype(F32)
    for d in (1, 2, 3):
        coords = coords + shift(part, "x", 4, d).astype(F32)
    correction = dot(coords.astype(BF), basis_rows, 1, 1)
    weight_t = (grad_t.astype(F32) - correction).astype(BF)
    got = []
    for s in range(8):
        owner = (z + s) % 8
        place = 2 * ((y - owner // 2) % 4) + ((owner % 2) ^ core)
        block_t = lax.dynamic_slice(weight_t, (0, 256 * place), (160, 256))
        got.append(shift(block_t, "z", 8, s) if s else block_t)
    got = jnp.stack(got)
    got = jnp.concatenate([lax.dynamic_index_in_dim(got, (z - o) % 8, 0, False) for o in range(8)], axis=0)
    weight_grad = got.T

    probe_part = dot(residual, test_matrix, 1, 0).astype(BF)
    probe = gather_small(sum_small(probe_part, COL, 8).astype(BF), COL, 8)
    sketch_part = dot(residual, probe, 0, 0).astype(BF)
    sketch = sum_small(sketch_part, TOK, 32)
    sketch_rows = gather_small(sketch, TOK, 32)
    gram_part = dot(sketch_rows, sketch_rows, 0, 0, precision=lax.Precision.HIGHEST)
    gram = gather_small(sum_small(gram_part, COL, 8), COL, 8) / D
    lower = jnp.linalg.cholesky(gram)
    sketch_basis = jax.scipy.linalg.solve_triangular(lower, sketch.T, lower=True).T
    return (weight_grad, sketch_basis)


def solution(mesh):
    grid = Mesh(mesh.devices.reshape(8, 4, 4, 2), ("z", "x", "y", "core"))
    return jax.shard_map(
        per_device,
        mesh=grid,
        in_specs=(P(TOK, None), P(TOK, COL), P(TOK, None), P(TOK, COL), P(COL, None)),
        out_specs=(P(TOK, COL), P(COL + TOK, None)),
        check_vma=False,
    )
```

```python
import jax
import jax.numpy as jnp
from jax import lax
from jax.sharding import Mesh, PartitionSpec as P

D = 8192
BF = jnp.bfloat16
F32 = jnp.float32
TOK = ("z", "x")
COL = ("y", "core")


def shift(a, axis, n, d):
    return lax.ppermute(a, axis, [(i, (i + d) % n) for i in range(n)])


def dot(a, b, ca, cb, **kw):
    return lax.dot_general(a, b, (((ca,), (cb,)), ((), ())), preferred_element_type=F32, **kw)


def exchange(a, axes):
    return lax.all_to_all(a, axes, split_axis=0, concat_axis=0, tiled=False)


def gather_small(a, axes, n):
    return exchange(jnp.broadcast_to(a[None], (n,) + a.shape), axes)


def total(parts):
    return jnp.sum(parts.astype(F32), axis=0)


def after(value, *others):
    return lax.optimization_barrier((value,) + others)[0]


def per_device(inputs, out_grads, basis, residual, test_matrix):
    z, x, y, core = (lax.axis_index(name) for name in ("z", "x", "y", "core"))
    col = 2 * y + core

    def block(d):
        return lax.dynamic_slice(inputs, (0, 1024 * col + 256 * ((x + d) % 4)), (512, 256))

    mine = jnp.concatenate([block(0)] + [shift(block(d), "x", 4, d) for d in (1, 2, 3)], axis=0)
    grads1 = shift(out_grads, "x", 4, 1)
    grads3 = shift(out_grads, "x", 4, -1)
    grads2 = [shift(grads1[:256], "x", 4, 1), shift(grads3[256:], "x", 4, -1)]
    basis_rows = lax.all_gather(basis, "z", axis=0, tiled=True)

    probe_part = dot(residual, test_matrix, 1, 0).astype(BF)
    probe_sum = total(exchange(probe_part.reshape(8, 64, 256), COL)).astype(BF)
    mine, probe_sum = lax.optimization_barrier((mine, probe_sum))

    rows_of = jnp.zeros((2048, 2048), BF)

    def place(rows_of, piece, e, f):
        owner = 2 * ((y - e) % 4) + (core ^ f)
        return lax.dynamic_update_slice(rows_of, piece, (0, 256 * owner))

    one = shift(mine, "y", 4, 1)
    three = shift(mine, "y", 4, -1)
    zero_b = shift(mine, "core", 2, 1)
    probe = gather_small(probe_sum, COL, 8).reshape(512, 256)
    sketch_part = dot(residual, probe, 0, 0).astype(BF)
    sketch_part = sketch_part.reshape(8, 4, 32, 256).transpose(1, 0, 2, 3)
    sketch_x = total(exchange(sketch_part, "x"))
    one, three, sketch_x = lax.optimization_barrier((one, three, sketch_x))
    top = shift(one[:1024], "y", 4, 1)
    bottom = shift(three[1024:], "y", 4, -1)
    one_b = shift(one, "core", 2, 1)
    three_b = shift(three, "core", 2, 1)
    sketch = total(exchange(sketch_x, "z"))
    two = jnp.concatenate([top, bottom], axis=0)
    two_b = shift(two, "core", 2, 1)
    for e, (own, other) in enumerate([(mine, zero_b), (one, one_b), (two, two_b), (three, three_b)]):
        rows_of = place(place(rows_of, own, e, 0), other, e, 1)
    grads = jnp.concatenate([out_grads, grads1] + grads2 + [grads3], axis=0)
    grads, sketch = lax.optimization_barrier((grads, sketch))

    part_t = dot(grads, rows_of, 0, 0).astype(BF)
    part_t, sketch = lax.optimization_barrier((part_t, sketch))
    grad_t = lax.psum_scatter(part_t, "z", scatter_dimension=0, tiled=True)

    gram_part = dot(sketch, sketch, 0, 0, precision=lax.Precision.HIGHEST)
    gram = total(exchange(gram_part.reshape(8, 32, 256), COL))
    gram = total(gather_small(gram, "x", 4))
    gram = total(gather_small(gram, "z", 8))
    gram = gather_small(gram, COL, 8).reshape(256, 256) / D
    lower = jnp.linalg.cholesky(gram)
    sketch_basis = jax.scipy.linalg.solve_triangular(lower, sketch.T, lower=True).T

    part = dot(grad_t, basis_rows, 1, 0).astype(BF)
    coords = total(gather_small(part, "x", 4)).astype(BF)
    correction = dot(coords, basis_rows, 1, 1)
    weight_t = (grad_t.astype(F32) - correction).astype(BF)
    weight_t = weight_t.reshape(160, 8, 256).transpose(1, 0, 2)
    weight_grad = exchange(weight_t, "z").reshape(1280, 256).T
    return (weight_grad, sketch_basis)


def solution(mesh):
    grid = Mesh(mesh.devices.reshape(8, 4, 4, 2), ("z", "x", "y", "core"))
    return jax.shard_map(
        per_device,
        mesh=grid,
        in_specs=(P(TOK, None), P(TOK, COL), P(TOK, None), P(TOK, COL), P(COL, None)),
        out_specs=(P(TOK, COL), P(COL + TOK, None)),
        check_vma=False,
    )
```

```python
import jax
import jax.numpy as jnp
from jax import lax
from jax.sharding import Mesh, PartitionSpec as P

D = 8192
BF = jnp.bfloat16
F32 = jnp.float32
TOK = ("z", "x")
COL = ("y", "core")


def shift(a, axis, n, d):
    return lax.ppermute(a, axis, [(i, (i + d) % n) for i in range(n)])


def dot(a, b, ca, cb, **kw):
    return lax.dot_general(a, b, (((ca,), (cb,)), ((), ())), preferred_element_type=F32, **kw)


def exchange(a, axes):
    return lax.all_to_all(a, axes, split_axis=0, concat_axis=0, tiled=False)


def gather_small(a, axes, n):
    return exchange(jnp.broadcast_to(a[None], (n,) + a.shape), axes)


def total(parts):
    return jnp.sum(parts.astype(F32), axis=0)


def solve_factor(gram, rows):
    n = gram.shape[0] // 2
    high = dict(precision=lax.Precision.HIGHEST)
    eye = jnp.eye(n, dtype=F32)

    def factor(a):
        lower = lax.linalg.cholesky(a, symmetrize_input=False)
        return lax.linalg.triangular_solve(lower, eye, left_side=True, lower=True)

    inverse1 = factor(gram[:n, :n])
    below = dot(gram[n:, :n], inverse1, 1, 1, **high)
    inverse2 = factor(gram[n:, n:] - dot(below, below, 1, 1, **high))
    first = dot(rows[:, :n], inverse1, 1, 1, **high)
    second = dot(rows[:, n:] - dot(first, below, 1, 1, **high), inverse2, 1, 1, **high)
    return jnp.concatenate([first, second], axis=1)


def per_device(inputs, out_grads, basis, residual, test_matrix):
    z, x, y, core = (lax.axis_index(name) for name in ("z", "x", "y", "core"))
    col = 2 * y + core

    def block(d):
        return lax.dynamic_slice(inputs, (0, 1024 * col + 256 * ((x + d) % 4)), (512, 256))

    mine = jnp.concatenate([block(0)] + [shift(block(d), "x", 4, d) for d in (1, 2, 3)], axis=0)
    grads1 = shift(out_grads, "x", 4, 1)
    grads3 = shift(out_grads, "x", 4, -1)
    grads2 = [shift(grads1[:256], "x", 4, 1), shift(grads3[256:], "x", 4, -1)]
    basis_rows = lax.all_gather(basis, "z", axis=0, tiled=True)
    grads = jnp.concatenate([out_grads, grads1] + grads2 + [grads3], axis=0)

    probe_part = dot(residual, test_matrix, 1, 0).astype(BF)
    probe_sum = total(exchange(probe_part.reshape(8, 64, 256), COL)).astype(BF)

    one = shift(mine, "y", 4, 1)
    three = shift(mine, "y", 4, -1)
    mine_b = shift(mine, "core", 2, 1)
    one, three, probe_sum = lax.optimization_barrier((one, three, probe_sum))
    top = shift(one[:1024], "y", 4, 1)
    bottom = shift(three[1024:], "y", 4, -1)
    one_b = shift(one, "core", 2, 1)
    three_b = shift(three, "core", 2, 1)
    probe = gather_small(probe_sum, COL, 8).reshape(512, 256)
    top, bottom, probe = lax.optimization_barrier((top, bottom, probe))
    two = jnp.concatenate([top, bottom], axis=0)
    two_b = shift(two, "core", 2, 1)

    part_t = jnp.zeros((1280, 2048), BF)
    for piece, e, f in (
        (mine, 0, 0),
        (mine_b, 0, 1),
        (one, 1, 0),
        (three, 3, 0),
        (one_b, 1, 1),
        (three_b, 3, 1),
        (two, 2, 0),
        (two_b, 2, 1),
    ):
        owner = 2 * ((y - e) % 4) + (core ^ f)
        part_t = lax.dynamic_update_slice(part_t, dot(grads, piece, 0, 0).astype(BF), (0, 256 * owner))
    part_t, probe = lax.optimization_barrier((part_t, probe))
    grad_t = lax.psum_scatter(part_t, "z", scatter_dimension=0, tiled=True)

    sketch_part = dot(residual, probe, 0, 0).astype(BF)
    sketch = total(exchange(sketch_part.reshape(8, 128, 256), "z"))
    sketch = total(exchange(sketch.reshape(4, 32, 256), "x"))
    gram_part = dot(sketch, sketch, 0, 0, precision=lax.Precision.HIGHEST)
    gram = total(exchange(gram_part.reshape(8, 32, 256), COL))
    gram = total(gather_small(gram, "x", 4))
    gram = total(gather_small(gram, "z", 8))
    gram = gather_small(gram, COL, 8).reshape(256, 256) / D
    sketch_basis = solve_factor(gram, sketch)

    part = dot(grad_t, basis_rows, 1, 0).astype(BF)
    coords = total(gather_small(part, "x", 4)).astype(BF)
    correction = dot(coords, basis_rows, 1, 1)
    weight_t = (grad_t.astype(F32) - correction).astype(BF)
    weight_t = weight_t.reshape(160, 8, 256).transpose(1, 0, 2)
    weight_grad = exchange(weight_t, "z").reshape(1280, 256).T
    return (weight_grad, sketch_basis)


def solution(mesh):
    grid = Mesh(mesh.devices.reshape(8, 4, 4, 2), ("z", "x", "y", "core"))
    return jax.shard_map(
        per_device,
        mesh=grid,
        in_specs=(P(TOK, None), P(TOK, COL), P(TOK, None), P(TOK, COL), P(COL, None)),
        out_specs=(P(TOK, COL), P(COL + TOK, None)),
        check_vma=False,
    )
```

```python
import jax
import jax.numpy as jnp
from jax import lax
from jax.experimental import pallas as pl
from jax.experimental.pallas import tpu as pltpu
from jax.sharding import Mesh, PartitionSpec as P

D = 8192
BF = jnp.bfloat16
F32 = jnp.float32
TOK = ("z", "x")
COL = ("y", "core")


def shift(a, axis, n, d):
    return lax.ppermute(a, axis, [(i, (i + d) % n) for i in range(n)])


def dot(a, b, ca, cb, **kw):
    return lax.dot_general(a, b, (((ca,), (cb,)), ((), ())), preferred_element_type=F32, **kw)


def exchange(a, axes):
    return lax.all_to_all(a, axes, split_axis=0, concat_axis=0, tiled=False)


def gather_small(a, axes, n):
    return exchange(jnp.broadcast_to(a[None], (n,) + a.shape), axes)


def total(parts):
    return jnp.sum(parts.astype(F32), axis=0)


def product_kernel(owners, *refs):
    grads, rows, out = refs[:5], refs[5:15], refs[15]
    joined, blocks, result, grad_sems, row_sems, out_sems = refs[16:]

    def columns(p):
        return pl.ds(256 * p, 256)

    places = [(0, 1280, 0), (0, 1280, 512), (0, 640, 1024), (640, 640, 1024), (0, 1280, 1536)]
    loads = [
        pltpu.make_async_copy(grads[i], joined.at[pl.ds(top, size), pl.ds(left, 512)], grad_sems.at[i])
        for i, (top, size, left) in enumerate(places)
    ]
    row_loads = [pltpu.make_async_copy(rows[p], blocks.at[:, columns(p)], row_sems.at[p]) for p in range(6)]
    for i in range(4):
        block, half = 6 + i // 2, i % 2
        row_loads.append(
            pltpu.make_async_copy(rows[6 + i], blocks.at[pl.ds(1024 * half, 1024), columns(block)], row_sems.at[6 + i])
        )
    for load in loads + row_loads:
        load.start()
    for load in loads:
        load.wait()
    stores = []
    for q in range(4):
        for load in row_loads[2 * q : 2 * q + 2] if q < 3 else row_loads[6:]:
            load.wait()
        pair = pl.ds(512 * q, 512)
        result[:, pair] = jnp.dot(joined[...], blocks[:, pair], preferred_element_type=F32).astype(BF)
        for p in (2 * q, 2 * q + 1):
            place = pl.ds(pl.multiple_of(256 * owners[p], 256), 256)
            stores.append(pltpu.make_async_copy(result.at[:, columns(p)], out.at[:, place], out_sems.at[p]))
            stores[-1].start()
    for store in stores:
        store.wait()


def product(owners, grads, rows):
    anywhere = pl.BlockSpec(memory_space=pl.ANY)
    return pl.pallas_call(
        product_kernel,
        out_shape=jax.ShapeDtypeStruct((1280, 2048), BF),
        grid_spec=pltpu.PrefetchScalarGridSpec(
            num_scalar_prefetch=1,
            grid=(1,),
            in_specs=[anywhere] * 15,
            out_specs=anywhere,
            scratch_shapes=[
                pltpu.VMEM((1280, 2048), BF),
                pltpu.VMEM((2048, 2048), BF),
                pltpu.VMEM((1280, 2048), BF),
                pltpu.SemaphoreType.DMA((5,)),
                pltpu.SemaphoreType.DMA((10,)),
                pltpu.SemaphoreType.DMA((8,)),
            ],
        ),
        compiler_params=pltpu.CompilerParams(vmem_limit_bytes=40 * 2**20),
    )(owners, *grads, *rows)


def solve_factor(gram, rows):
    n = gram.shape[0] // 2
    high = dict(precision=lax.Precision.HIGHEST)
    eye = jnp.eye(n, dtype=F32)

    def factor(a):
        lower = lax.linalg.cholesky(a, symmetrize_input=False)
        return lax.linalg.triangular_solve(lower, eye, left_side=True, lower=True)

    inverse1 = factor(gram[:n, :n])
    below = dot(gram[n:, :n], inverse1, 1, 1, **high)
    inverse2 = factor(gram[n:, n:] - dot(below, below, 1, 1, **high))
    first = dot(rows[:, :n], inverse1, 1, 1, **high)
    second = dot(rows[:, n:] - dot(first, below, 1, 1, **high), inverse2, 1, 1, **high)
    return jnp.concatenate([first, second], axis=1)


def per_device(inputs, out_grads, basis, residual, test_matrix):
    z, x, y, core = (lax.axis_index(name) for name in ("z", "x", "y", "core"))
    col = 2 * y + core

    def block(d):
        return lax.dynamic_slice(inputs, (0, 1024 * col + 256 * ((x + d) % 4)), (512, 256))

    mine = jnp.concatenate([block(0)] + [shift(block(d), "x", 4, d) for d in (1, 2, 3)], axis=0)
    grads0 = out_grads.T
    grads1 = shift(grads0, "x", 4, 1)
    grads3 = shift(grads0, "x", 4, -1)
    grads2 = [shift(grads1[:640], "x", 4, 1), shift(grads3[640:], "x", 4, -1)]
    basis_rows = lax.all_gather(basis, "z", axis=0, tiled=True)

    probe_part = dot(residual, test_matrix, 1, 0).astype(BF)
    probe_sum = total(exchange(probe_part.reshape(8, 64, 256), COL)).astype(BF)
    mine, probe_sum = lax.optimization_barrier((mine, probe_sum))
    one = shift(mine, "y", 4, 1)
    three = shift(mine, "y", 4, -1)
    mine_b = shift(mine, "core", 2, 1)
    probe = gather_small(probe_sum, COL, 8).reshape(512, 256)
    one, three, probe = lax.optimization_barrier((one, three, probe))
    top = shift(one[:1024], "y", 4, 1)
    bottom = shift(three[1024:], "y", 4, -1)
    one_b = shift(one, "core", 2, 1)
    three_b = shift(three, "core", 2, 1)
    sketch_part = dot(residual, probe, 0, 0).astype(BF)
    sketch = total(exchange(sketch_part.reshape(8, 128, 256), "z"))
    top, bottom, sketch = lax.optimization_barrier((top, bottom, sketch))
    top_b = shift(top, "core", 2, 1)
    bottom_b = shift(bottom, "core", 2, 1)

    owners = jnp.stack([2 * ((y - e) % 4) + (core ^ f) for e in (0, 1, 3, 2) for f in (0, 1)]).astype(jnp.int32)
    part_t = product(
        owners,
        [grads0, grads1] + grads2 + [grads3],
        [mine, mine_b, one, one_b, three, three_b, top, bottom, top_b, bottom_b],
    )
    part_t, sketch = lax.optimization_barrier((part_t, sketch))
    grad_t = lax.psum_scatter(part_t, "z", scatter_dimension=0, tiled=True)

    sketch = total(exchange(sketch.reshape(4, 32, 256), "x"))
    gram_part = dot(sketch, sketch, 0, 0, precision=lax.Precision.HIGHEST)
    gram = total(exchange(gram_part.reshape(8, 32, 256), COL))
    gram = total(exchange(gram.reshape(4, 8, 256), "x"))
    gram = total(gather_small(gram, "z", 8))
    gram = gather_small(gram, ("y", "core", "x"), 32).reshape(256, 256) / D
    sketch_basis = solve_factor(gram, sketch)

    part = dot(grad_t, basis_rows, 1, 0).astype(BF)
    coords = total(gather_small(part, "x", 4)).astype(BF)
    correction = dot(coords, basis_rows, 1, 1)
    weight_t = (grad_t.astype(F32) - correction).astype(BF)
    weight_t = weight_t.reshape(160, 8, 256).transpose(1, 0, 2)
    weight_grad = exchange(weight_t, "z").reshape(1280, 256).T
    return (weight_grad, sketch_basis)


def solution(mesh):
    grid = Mesh(mesh.devices.reshape(8, 4, 4, 2), ("z", "x", "y", "core"))
    return jax.shard_map(
        per_device,
        mesh=grid,
        in_specs=(P(TOK, None), P(TOK, COL), P(TOK, None), P(TOK, COL), P(COL, None)),
        out_specs=(P(TOK, COL), P(COL + TOK, None)),
        check_vma=False,
    )
```

```python
import jax
import jax.numpy as jnp
from jax import lax
from jax.experimental import pallas as pl
from jax.experimental.pallas import tpu as pltpu
from jax.sharding import Mesh, PartitionSpec as P

D = 8192
BF = jnp.bfloat16
F32 = jnp.float32
TOK = ("z", "x")
COL = ("y", "core")


def shift(a, axis, n, d):
    return lax.ppermute(a, axis, [(i, (i + d) % n) for i in range(n)])


def dot(a, b, ca, cb, **kw):
    return lax.dot_general(a, b, (((ca,), (cb,)), ((), ())), preferred_element_type=F32, **kw)


def exchange(a, axes):
    return lax.all_to_all(a, axes, split_axis=0, concat_axis=0, tiled=False)


def gather_small(a, axes, n):
    return exchange(jnp.broadcast_to(a[None], (n,) + a.shape), axes)


def total(parts):
    return jnp.sum(parts.astype(F32), axis=0)


def product_kernel(owners, *refs):
    grads, rows, out = refs[:5], refs[5:15], refs[15]
    joined, blocks, result, grad_sems, row_sems, out_sems = refs[16:]

    def columns(p):
        return pl.ds(256 * p, 256)

    places = [(0, 1280, 0), (0, 1280, 512), (0, 640, 1024), (640, 640, 1024), (0, 1280, 1536)]
    loads = [
        pltpu.make_async_copy(grads[i], joined.at[pl.ds(top, size), pl.ds(left, 512)], grad_sems.at[i])
        for i, (top, size, left) in enumerate(places)
    ]
    row_loads = [pltpu.make_async_copy(rows[p], blocks.at[:, columns(p)], row_sems.at[p]) for p in range(6)]
    for i in range(4):
        block, half = 6 + i // 2, i % 2
        row_loads.append(
            pltpu.make_async_copy(rows[6 + i], blocks.at[pl.ds(1024 * half, 1024), columns(block)], row_sems.at[6 + i])
        )
    for load in loads + row_loads:
        load.start()
    for load in loads:
        load.wait()
    stores = []
    for q in range(4):
        for load in row_loads[2 * q : 2 * q + 2] if q < 3 else row_loads[6:]:
            load.wait()
        pair = pl.ds(512 * q, 512)
        result[:, pair] = jnp.dot(joined[...], blocks[:, pair], preferred_element_type=F32).astype(BF)
        for p in (2 * q, 2 * q + 1):
            place = pl.ds(pl.multiple_of(256 * owners[p], 256), 256)
            stores.append(pltpu.make_async_copy(result.at[:, columns(p)], out.at[:, place], out_sems.at[p]))
            stores[-1].start()
    for store in stores:
        store.wait()


def product(owners, grads, rows):
    anywhere = pl.BlockSpec(memory_space=pl.ANY)
    return pl.pallas_call(
        product_kernel,
        out_shape=jax.ShapeDtypeStruct((1280, 2048), BF),
        grid_spec=pltpu.PrefetchScalarGridSpec(
            num_scalar_prefetch=1,
            grid=(1,),
            in_specs=[anywhere] * 15,
            out_specs=anywhere,
            scratch_shapes=[
                pltpu.VMEM((1280, 2048), BF),
                pltpu.VMEM((2048, 2048), BF),
                pltpu.VMEM((1280, 2048), BF),
                pltpu.SemaphoreType.DMA((5,)),
                pltpu.SemaphoreType.DMA((10,)),
                pltpu.SemaphoreType.DMA((8,)),
            ],
        ),
        compiler_params=pltpu.CompilerParams(vmem_limit_bytes=40 * 2**20),
    )(owners, *grads, *rows)


def solve_factor(gram, rows, first_value):
    n = gram.shape[0] // 2
    high = dict(precision=lax.Precision.HIGHEST)
    eye = jnp.eye(n, dtype=F32)

    def factor(a):
        lower = lax.linalg.cholesky(a, symmetrize_input=False)
        return lax.linalg.triangular_solve(lower, eye, left_side=True, lower=True)

    inverse1 = factor(gram[:n, :n])
    below = dot(gram[n:, :n], inverse1, 1, 1, **high)
    rest = gram[n:, n:] - dot(below, below, 1, 1, **high)
    rest, first_value = lax.optimization_barrier((rest, first_value))
    inverse2 = factor(rest)
    first = dot(rows[:, :n], inverse1, 1, 1, **high)
    second = dot(rows[:, n:] - dot(first, below, 1, 1, **high), inverse2, 1, 1, **high)
    return jnp.concatenate([first, second], axis=1), first_value


def per_device(inputs, out_grads, basis, residual, test_matrix):
    z, x, y, core = (lax.axis_index(name) for name in ("z", "x", "y", "core"))
    col = 2 * y + core

    probe_part = dot(residual, test_matrix, 1, 0).astype(BF)
    inputs, probe_part = lax.optimization_barrier((inputs, probe_part))
    probe_sum = total(exchange(probe_part.reshape(8, 64, 256), COL)).astype(BF)
    probe = gather_small(probe_sum, COL, 8).reshape(512, 256)

    def block(d):
        return lax.dynamic_slice(inputs, (0, 1024 * col + 256 * ((x + d) % 4)), (512, 256))

    mine = jnp.concatenate([block(0)] + [shift(block(d), "x", 4, d) for d in (1, 2, 3)], axis=0)
    grads0 = out_grads.T
    grads1 = shift(grads0, "x", 4, 1)
    grads3 = shift(grads0, "x", 4, -1)
    basis_rows = lax.all_gather(basis, "z", axis=0, tiled=True)

    mine, probe = lax.optimization_barrier((mine, probe))
    one = shift(mine, "y", 4, 1)
    three = shift(mine, "y", 4, -1)
    mine_b = shift(mine, "core", 2, 1)
    probe, mine_b, grads1, grads3 = lax.optimization_barrier((probe, mine_b, grads1, grads3))
    sketch_part = dot(residual, probe, 0, 0).astype(BF)
    sketch = total(exchange(sketch_part.reshape(8, 128, 256), "z"))
    top = shift(one[:1024], "y", 4, 1)
    bottom = shift(three[1024:], "y", 4, -1)
    grads2 = [shift(grads1[:640], "x", 4, 1), shift(grads3[640:], "x", 4, -1)]
    one_b = shift(one, "core", 2, 1)
    three_b = shift(three, "core", 2, 1)
    top, bottom, sketch = lax.optimization_barrier((top, bottom, sketch))
    top_b = shift(top, "core", 2, 1)
    bottom_b = shift(bottom, "core", 2, 1)

    owners = jnp.stack([2 * ((y - e) % 4) + (core ^ f) for e in (0, 1, 3, 2) for f in (0, 1)]).astype(jnp.int32)
    part_t = product(
        owners,
        [grads0, grads1] + grads2 + [grads3],
        [mine, mine_b, one, one_b, three, three_b, top, bottom, top_b, bottom_b],
    )
    part_t, sketch = lax.optimization_barrier((part_t, sketch))
    grad_t = lax.psum_scatter(part_t, "z", scatter_dimension=0, tiled=True)

    rows = total(gather_small(sketch, "x", 4))
    sketch = lax.dynamic_slice(rows, (32 * x, 0), (32, 256))
    gram_part = dot(rows, rows, 0, 0, precision=lax.Precision.HIGHEST)
    gram = total(exchange(gram_part.reshape(8, 32, 256), COL))
    gram = total(gather_small(lax.dynamic_slice(gram, (8 * x, 0), (8, 256)), "z", 8))
    gram = gather_small(gram, ("y", "core", "x"), 32).reshape(256, 256) / D

    part = dot(grad_t, basis_rows, 1, 0).astype(BF)
    coords = total(gather_small(part, "x", 4)).astype(BF)
    correction = dot(coords, basis_rows, 1, 1)
    weight_t = (grad_t.astype(F32) - correction).astype(BF)
    weight_t = weight_t.reshape(160, 8, 256).transpose(1, 0, 2)
    sketch_basis, weight_t = solve_factor(gram, sketch, weight_t)
    weight_grad = exchange(weight_t, "z").reshape(1280, 256).T
    return (weight_grad, sketch_basis)


def solution(mesh):
    grid = Mesh(mesh.devices.reshape(8, 4, 4, 2), ("z", "x", "y", "core"))
    return jax.shard_map(
        per_device,
        mesh=grid,
        in_specs=(P(TOK, None), P(TOK, COL), P(TOK, None), P(TOK, COL), P(COL, None)),
        out_specs=(P(TOK, COL), P(COL + TOK, None)),
        check_vma=False,
    )
```

```python
import jax
import jax.numpy as jnp
from jax import lax
from jax.experimental import pallas as pl
from jax.experimental.pallas import tpu as pltpu
from jax.sharding import Mesh, PartitionSpec as P

D = 8192
BF = jnp.bfloat16
F32 = jnp.float32
TOK = ("z", "x")
COL = ("y", "core")


def shift(a, axis, n, d):
    return lax.ppermute(a, axis, [(i, (i + d) % n) for i in range(n)])


def dot(a, b, ca, cb, **kw):
    return lax.dot_general(a, b, (((ca,), (cb,)), ((), ())), preferred_element_type=F32, **kw)


def exchange(a, axes):
    return lax.all_to_all(a, axes, split_axis=0, concat_axis=0, tiled=False)


def gather_small(a, axes, n):
    return exchange(jnp.broadcast_to(a[None], (n,) + a.shape), axes)


def total(parts):
    return jnp.sum(parts.astype(F32), axis=0)


def product_kernel(owners, *refs):
    grads, rows, out = refs[:5], refs[5:15], refs[15]
    joined, blocks, result, grad_sems, row_sems, out_sems = refs[16:]

    def columns(p):
        return pl.ds(256 * p, 256)

    places = [(0, 1280, 0), (0, 1280, 512), (0, 640, 1024), (640, 640, 1024), (0, 1280, 1536)]
    loads = [
        pltpu.make_async_copy(grads[i], joined.at[pl.ds(top, size), pl.ds(left, 512)], grad_sems.at[i])
        for i, (top, size, left) in enumerate(places)
    ]
    row_loads = [pltpu.make_async_copy(rows[p], blocks.at[:, columns(p)], row_sems.at[p]) for p in range(6)]
    for i in range(4):
        block, half = 6 + i // 2, i % 2
        row_loads.append(
            pltpu.make_async_copy(rows[6 + i], blocks.at[pl.ds(1024 * half, 1024), columns(block)], row_sems.at[6 + i])
        )
    for load in loads + row_loads:
        load.start()
    for load in loads:
        load.wait()
    stores = []
    for q in range(4):
        for load in row_loads[2 * q : 2 * q + 2] if q < 3 else row_loads[6:]:
            load.wait()
        pair = pl.ds(512 * q, 512)
        result[:, pair] = jnp.dot(joined[...], blocks[:, pair], preferred_element_type=F32).astype(BF)
        for p in (2 * q, 2 * q + 1):
            place = pl.ds(pl.multiple_of(256 * owners[p], 256), 256)
            stores.append(pltpu.make_async_copy(result.at[:, columns(p)], out.at[:, place], out_sems.at[p]))
            stores[-1].start()
    for store in stores:
        store.wait()


def product(owners, grads, rows):
    anywhere = pl.BlockSpec(memory_space=pl.ANY)
    return pl.pallas_call(
        product_kernel,
        out_shape=jax.ShapeDtypeStruct((1280, 2048), BF),
        grid_spec=pltpu.PrefetchScalarGridSpec(
            num_scalar_prefetch=1,
            grid=(1,),
            in_specs=[anywhere] * 15,
            out_specs=anywhere,
            scratch_shapes=[
                pltpu.VMEM((1280, 2048), BF),
                pltpu.VMEM((2048, 2048), BF),
                pltpu.VMEM((1280, 2048), BF),
                pltpu.SemaphoreType.DMA((5,)),
                pltpu.SemaphoreType.DMA((10,)),
                pltpu.SemaphoreType.DMA((8,)),
            ],
        ),
        compiler_params=pltpu.CompilerParams(vmem_limit_bytes=40 * 2**20),
    )(owners, *grads, *rows)


def solve_factor(gram, rows, first_value):
    n = gram.shape[0] // 2
    high = dict(precision=lax.Precision.HIGHEST)
    eye = jnp.eye(n, dtype=F32)

    def factor(a):
        lower = lax.linalg.cholesky(a, symmetrize_input=False)
        return lax.linalg.triangular_solve(lower, eye, left_side=True, lower=True)

    inverse1 = factor(gram[:n, :n])
    below = dot(gram[n:, :n], inverse1, 1, 1, **high)
    rest = gram[n:, n:] - dot(below, below, 1, 1, **high)
    rest, first_value = lax.optimization_barrier((rest, first_value))
    inverse2 = factor(rest)
    first = dot(rows[:, :n], inverse1, 1, 1, **high)
    second = dot(rows[:, n:] - dot(first, below, 1, 1, **high), inverse2, 1, 1, **high)
    return jnp.concatenate([first, second], axis=1), first_value


def per_device(inputs, out_grads, basis, residual, test_matrix):
    z, x, y, core = (lax.axis_index(name) for name in ("z", "x", "y", "core"))
    col = 2 * y + core

    probe_part = dot(residual, test_matrix, 1, 0).astype(BF)
    inputs, probe_part = lax.optimization_barrier((inputs, probe_part))
    probe_sum = total(exchange(probe_part.reshape(8, 64, 256), COL)).astype(BF)
    probe = gather_small(probe_sum, COL, 8).reshape(512, 256)

    def block(d):
        return lax.dynamic_slice(inputs, (0, 1024 * col + 256 * ((x + d) % 4)), (512, 256))

    mine = jnp.concatenate([block(0)] + [shift(block(d), "x", 4, d) for d in (1, 2, 3)], axis=0)
    grads0 = out_grads.T
    grads1 = shift(grads0, "x", 4, 1)
    grads3 = shift(grads0, "x", 4, -1)
    basis_rows = lax.all_gather(basis, "z", axis=0, tiled=True)

    mine, probe = lax.optimization_barrier((mine, probe))
    one = shift(mine, "y", 4, 1)
    three = shift(mine, "y", 4, -1)
    mine_b = shift(mine, "core", 2, 1)
    probe, mine_b, grads1, grads3 = lax.optimization_barrier((probe, mine_b, grads1, grads3))
    sketch_part = dot(residual, probe, 0, 0).astype(BF)
    sketch = total(exchange(sketch_part.reshape(8, 128, 256), "z"))
    top = shift(one[:1024], "y", 4, 1)
    bottom = shift(three[1024:], "y", 4, -1)
    grads2 = [shift(grads1[:640], "x", 4, 1), shift(grads3[640:], "x", 4, -1)]
    one, grads2[0] = lax.optimization_barrier((one, grads2[0]))
    three, grads2[1] = lax.optimization_barrier((three, grads2[1]))
    one_b = shift(one, "core", 2, 1)
    three_b = shift(three, "core", 2, 1)
    top, bottom, sketch, *grads2 = lax.optimization_barrier((top, bottom, sketch, *grads2))
    top_b = shift(top, "core", 2, 1)
    bottom_b = shift(bottom, "core", 2, 1)

    owners = jnp.stack([2 * ((y - e) % 4) + (core ^ f) for e in (0, 1, 3, 2) for f in (0, 1)]).astype(jnp.int32)
    part_t = product(
        owners,
        [grads0, grads1] + grads2 + [grads3],
        [mine, mine_b, one, one_b, three, three_b, top, bottom, top_b, bottom_b],
    )
    part_t, sketch = lax.optimization_barrier((part_t, sketch))
    grad_t = lax.psum_scatter(part_t, "z", scatter_dimension=0, tiled=True)

    rows = total(gather_small(sketch, "x", 4))
    sketch = lax.dynamic_slice(rows, (32 * x, 0), (32, 256))
    gram_part = dot(rows, rows, 0, 0, precision=lax.Precision.HIGHEST)
    gram = total(exchange(gram_part.reshape(8, 32, 256), COL))
    gram = total(gather_small(lax.dynamic_slice(gram, (8 * x, 0), (8, 256)), "z", 8))
    gram = gather_small(gram, ("y", "core", "x"), 32).reshape(256, 256) / D

    part = dot(grad_t, basis_rows, 1, 0).astype(BF)
    coords = total(gather_small(part, "x", 4)).astype(BF)
    correction = dot(coords, basis_rows, 1, 1)
    weight_t = (grad_t.astype(F32) - correction).astype(BF)
    weight_t = weight_t.reshape(160, 8, 256).transpose(1, 0, 2)
    sketch_basis, weight_t = solve_factor(gram, sketch, weight_t)
    weight_grad = exchange(weight_t, "z").reshape(1280, 256).T
    return (weight_grad, sketch_basis)


def solution(mesh):
    grid = Mesh(mesh.devices.reshape(8, 4, 4, 2), ("z", "x", "y", "core"))
    return jax.shard_map(
        per_device,
        mesh=grid,
        in_specs=(P(TOK, None), P(TOK, COL), P(TOK, None), P(TOK, COL), P(COL, None)),
        out_specs=(P(TOK, COL), P(COL + TOK, None)),
        check_vma=False,
    )
```

```python
import jax
import jax.numpy as jnp
from jax import lax
from jax.experimental import pallas as pl
from jax.experimental.pallas import tpu as pltpu
from jax.sharding import Mesh, PartitionSpec as P

D = 8192
BF = jnp.bfloat16
F32 = jnp.float32
TOK = ("z", "x")
COL = ("y", "core")


def shift(a, axis, n, d):
    return lax.ppermute(a, axis, [(i, (i + d) % n) for i in range(n)])


def dot(a, b, ca, cb, **kw):
    return lax.dot_general(a, b, (((ca,), (cb,)), ((), ())), preferred_element_type=F32, **kw)


def exchange(a, axes):
    return lax.all_to_all(a, axes, split_axis=0, concat_axis=0, tiled=False)


def gather_small(a, axes, n):
    return exchange(jnp.broadcast_to(a[None], (n,) + a.shape), axes)


def total(parts):
    return jnp.sum(parts.astype(F32), axis=0)


def product_kernel(owners, *refs):
    grads, rows, out = refs[:5], refs[5:15], refs[15]
    joined, blocks, result, grad_sems, row_sems, out_sems = refs[16:]

    def columns(p):
        return pl.ds(256 * p, 256)

    places = [(0, 1280, 0), (0, 1280, 512), (0, 640, 1024), (640, 640, 1024), (0, 1280, 1536)]
    loads = [
        pltpu.make_async_copy(grads[i], joined.at[pl.ds(top, size), pl.ds(left, 512)], grad_sems.at[i])
        for i, (top, size, left) in enumerate(places)
    ]
    row_loads = [pltpu.make_async_copy(rows[p], blocks.at[:, columns(p)], row_sems.at[p]) for p in range(6)]
    for i in range(4):
        block, half = 6 + i // 2, i % 2
        row_loads.append(
            pltpu.make_async_copy(rows[6 + i], blocks.at[pl.ds(1024 * half, 1024), columns(block)], row_sems.at[6 + i])
        )
    for load in loads + row_loads:
        load.start()
    for load in loads:
        load.wait()
    stores = []
    for q in range(4):
        for load in row_loads[2 * q : 2 * q + 2] if q < 3 else row_loads[6:]:
            load.wait()
        pair = pl.ds(512 * q, 512)
        result[:, pair] = jnp.dot(joined[...], blocks[:, pair], preferred_element_type=F32).astype(BF)
        for p in (2 * q, 2 * q + 1):
            place = pl.ds(pl.multiple_of(256 * owners[p], 256), 256)
            stores.append(pltpu.make_async_copy(result.at[:, columns(p)], out.at[:, place], out_sems.at[p]))
            stores[-1].start()
    for store in stores:
        store.wait()


def product(owners, grads, rows):
    anywhere = pl.BlockSpec(memory_space=pl.ANY)
    return pl.pallas_call(
        product_kernel,
        out_shape=jax.ShapeDtypeStruct((1280, 2048), BF),
        grid_spec=pltpu.PrefetchScalarGridSpec(
            num_scalar_prefetch=1,
            grid=(1,),
            in_specs=[anywhere] * 15,
            out_specs=anywhere,
            scratch_shapes=[
                pltpu.VMEM((1280, 2048), BF),
                pltpu.VMEM((2048, 2048), BF),
                pltpu.VMEM((1280, 2048), BF),
                pltpu.SemaphoreType.DMA((5,)),
                pltpu.SemaphoreType.DMA((10,)),
                pltpu.SemaphoreType.DMA((8,)),
            ],
        ),
        compiler_params=pltpu.CompilerParams(vmem_limit_bytes=40 * 2**20),
    )(owners, *grads, *rows)


def solve_factor(gram, rows, first_value):
    n = gram.shape[0] // 2
    high = dict(precision=lax.Precision.HIGHEST)
    eye = jnp.eye(n, dtype=F32)

    def factor(a):
        lower = lax.linalg.cholesky(a, symmetrize_input=False)
        return lax.linalg.triangular_solve(lower, eye, left_side=True, lower=True)

    inverse1 = factor(gram[:n, :n])
    below = dot(gram[n:, :n], inverse1, 1, 1, **high)
    rest = gram[n:, n:] - dot(below, below, 1, 1, **high)
    rest, first_value = lax.optimization_barrier((rest, first_value))
    inverse2 = factor(rest)
    first = dot(rows[:, :n], inverse1, 1, 1, **high)
    second = dot(rows[:, n:] - dot(first, below, 1, 1, **high), inverse2, 1, 1, **high)
    return jnp.concatenate([first, second], axis=1), first_value


def per_device(inputs, out_grads, basis, residual, test_matrix):
    z, x, y, core = (lax.axis_index(name) for name in ("z", "x", "y", "core"))
    col = 2 * y + core

    probe_part = dot(residual, test_matrix, 1, 0).astype(BF)
    inputs, probe_part = lax.optimization_barrier((inputs, probe_part))
    probe_sum = total(exchange(probe_part.reshape(8, 64, 256), COL)).astype(BF)
    probe = gather_small(probe_sum, COL, 8).reshape(512, 256)

    def block(d):
        return lax.dynamic_slice(inputs, (0, 1024 * col + 256 * ((x + d) % 4)), (512, 256))

    mine = jnp.concatenate([block(0)] + [shift(block(d), "x", 4, d) for d in (1, 2, 3)], axis=0)
    grads0 = out_grads.T
    grads1 = shift(grads0, "x", 4, 1)
    grads3 = shift(grads0, "x", 4, -1)
    basis_rows = lax.all_gather(basis, "z", axis=0, tiled=True)

    mine, probe = lax.optimization_barrier((mine, probe))
    one = shift(mine, "y", 4, 1)
    three = shift(mine, "y", 4, -1)
    mine_b = shift(mine, "core", 2, 1)
    probe, mine_b, grads1, grads3, one, three = lax.optimization_barrier((probe, mine_b, grads1, grads3, one, three))
    sketch_part = dot(residual, probe, 0, 0).astype(BF)
    sketch = total(exchange(sketch_part.reshape(8, 128, 256), "z"))
    top = shift(one[:1024], "y", 4, 1)
    bottom = shift(three[1024:], "y", 4, -1)
    grads2 = [shift(grads1[:640], "x", 4, 1), shift(grads3[640:], "x", 4, -1)]
    one, grads2[0] = lax.optimization_barrier((one, grads2[0]))
    three, grads2[1] = lax.optimization_barrier((three, grads2[1]))
    one_b = shift(one, "core", 2, 1)
    three_b = shift(three, "core", 2, 1)
    top, bottom, sketch, *grads2 = lax.optimization_barrier((top, bottom, sketch, *grads2))
    top_b = shift(top, "core", 2, 1)
    bottom_b = shift(bottom, "core", 2, 1)

    owners = jnp.stack([2 * ((y - e) % 4) + (core ^ f) for e in (0, 1, 3, 2) for f in (0, 1)]).astype(jnp.int32)
    part_t = product(
        owners,
        [grads0, grads1] + grads2 + [grads3],
        [mine, mine_b, one, one_b, three, three_b, top, bottom, top_b, bottom_b],
    )
    part_t, sketch = lax.optimization_barrier((part_t, sketch))
    grad_t = lax.psum_scatter(part_t, "z", scatter_dimension=0, tiled=True)

    rows = total(gather_small(sketch, "x", 4))
    sketch = lax.dynamic_slice(rows, (32 * x, 0), (32, 256))
    gram_part = dot(rows, rows, 0, 0, precision=lax.Precision.HIGHEST)
    gram = total(exchange(gram_part.reshape(8, 32, 256), COL))
    gram = total(gather_small(lax.dynamic_slice(gram, (8 * x, 0), (8, 256)), "z", 8))
    gram = gather_small(gram, ("y", "core", "x"), 32).reshape(256, 256) / D

    part = dot(grad_t, basis_rows, 1, 0).astype(BF)
    coords = total(gather_small(part, "x", 4)).astype(BF)
    correction = dot(coords, basis_rows, 1, 1)
    weight_t = (grad_t.astype(F32) - correction).astype(BF)
    weight_t = weight_t.reshape(160, 8, 256).transpose(1, 0, 2)
    sketch_basis, weight_t = solve_factor(gram, sketch, weight_t)
    weight_grad = exchange(weight_t, "z").reshape(1280, 256).T
    return (weight_grad, sketch_basis)


def solution(mesh):
    grid = Mesh(mesh.devices.reshape(8, 4, 4, 2), ("z", "x", "y", "core"))
    return jax.shard_map(
        per_device,
        mesh=grid,
        in_specs=(P(TOK, None), P(TOK, COL), P(TOK, None), P(TOK, COL), P(COL, None)),
        out_specs=(P(TOK, COL), P(COL + TOK, None)),
        check_vma=False,
    )
```
